512 devices in a mesh: wide: 32 (over x, z_lo), narrow: 16 (over z_hi, y, core).
Axes of the slice: x: 4, y: 4, z: 16 (z_hi: 2, z_lo: 8; z = z_hi * 8 + z_lo), core: 2. Of those that a mesh axis runs over, the one named last changes fastest.
Arguments:
- grad: bfloat16 [4096, 4096], P('narrow', 'wide'), may hold values from -6 to 6
- moment: float32 [4096, 4096], P('narrow', 'wide'), may hold values from -4 to 4
- second: float32 [4096, 4096], P('narrow', 'wide'), may hold values from 0.05 to 2
- left_basis: bfloat16 [4096, 4096], P('wide', 'narrow'), may hold values from -0.09375 to 0.09375
- right_basis: bfloat16 [4096, 4096], P('narrow', 'wide'), may hold values from -0.09375 to 0.09375
Outputs:
- moment_new: float32 [4096, 4096], P('narrow', 'wide')
- second_new: float32 [4096, 4096], P('narrow', 'wide')
- update: bfloat16 [4096, 4096], P('narrow', 'wide')
The draws below stay inside these ranges and needn't reach their ends.
All inputs are finite; a program needn't handle non-finite values.
Results may differ from the reference program's by a relative error of at most 0.027.
Values may be sent and summed in bfloat16 or wider, within the bound.
No kernel may reach another device: no remote copies, remote signals or barrier semaphores. Data moves between devices by JAX's collectives and lax.ppermute only.
A program may use at most 64 MiB of HBM per device.

```python
import math
import jax
import jax.numpy as jnp
from jax import lax

KL = 4096
KR = 4096
STEP = 10
N_WIDE = 32
N_NARROW = 16


def levels(rng, dims, cuts, least, largest):
    loudness = 1.0
    for position, shards_of in cuts:
        heights = jax.random.uniform(jax.random.fold_in(jax.random.fold_in(rng, 6), position), (shards_of,), jnp.float32, least / len(cuts), largest / len(cuts))
        loudness = loudness * jnp.repeat(jnp.exp(heights), dims[position] // shards_of).reshape((-1,) + (1,) * (len(dims) - 1 - position))
    return loudness


def normal_values(own_key, shape, deviation, limit, cuts=(), dtype=jnp.bfloat16):
    loudness = levels(own_key, shape, cuts, -0.22, 0.18) if cuts else 1.0
    array = jax.random.normal(own_key, shape, jnp.float32) * deviation * loudness
    return jnp.minimum(jnp.maximum(array, -limit), limit).astype(dtype)


def setup_inputs(seed: int = 0) -> dict:
    key_of = jax.random.split(jax.random.key(seed), 6)
    return {
        "grad": normal_values(key_of[0], (KL, KR), 1.0, 6.0, ((0, 16), (1, 32))),
        "moment": normal_values(key_of[1], (KL, KR), 0.5, 4.0, ((0, 16), (1, 32)), jnp.float32),
        "second": jnp.clip(jnp.exp(math.log(2.0) - 3.6888794 * jax.random.uniform(key_of[2], (KL, KR), jnp.float32) ** levels(key_of[2], (KL, KR), ((0, 16), (1, 32)), -0.2, 0.2)), 0.05, 2.0),
        "left_basis": normal_values(key_of[3], (KL, KL), KL ** -0.5, 0.09375, ((0, 32), (1, 16))),
        "right_basis": normal_values(key_of[4], (KR, KR), KR ** -0.5, 0.09375, ((0, 16), (1, 32))),
    }


beta_first = 0.95
beta_second = 0.95
epsilon = 1e-08

def reference(grad, moment, second, left_basis, right_basis):
    moment_new = beta_first * moment + (1.0 - beta_first) * grad.astype(jnp.float32)
    moment_low = moment_new.astype(jnp.bfloat16)
    right_grad = jnp.dot(grad, right_basis, preferred_element_type=jnp.float32).astype(jnp.bfloat16)
    right_moment = jnp.dot(moment_low, right_basis, preferred_element_type=jnp.float32).astype(jnp.bfloat16)
    grad_rot = jnp.dot(left_basis.T, right_grad, preferred_element_type=jnp.float32)
    moment_rot = jnp.dot(left_basis.T, right_moment, preferred_element_type=jnp.float32)
    second_new = beta_second * second + (1.0 - beta_second) * grad_rot * grad_rot
    bias_first = 1.0 - beta_first ** STEP
    bias_second = 1.0 - beta_second ** STEP
    normed = (moment_rot / bias_first / (jnp.sqrt(second_new / bias_second) + epsilon)).astype(jnp.bfloat16)
    wide_block = KR // N_WIDE

    def spectral_step(index, totals):
        begin = (index * wide_block).astype(jnp.int32)
        normed_block = lax.dynamic_slice_in_dim(normed, begin, wide_block, 1)
        basis_block = lax.dynamic_slice_in_dim(right_basis, begin, wide_block, 1)
        term = jnp.dot(normed_block, basis_block.T, preferred_element_type=jnp.float32).astype(jnp.bfloat16)
        term = lax.optimization_barrier(term)
        return totals + term.astype(jnp.float32)
    spectral = lax.fori_loop(0, N_WIDE, spectral_step, jnp.zeros((KL, KR), jnp.float32))
    spectral_low = spectral.astype(jnp.bfloat16)
    narrow_block = KL // N_NARROW

    def basis_step(index, totals):
        begin = (index * narrow_block).astype(jnp.int32)
        basis_block = lax.dynamic_slice_in_dim(left_basis, begin, narrow_block, 1)
        spectral_block = lax.dynamic_slice_in_dim(spectral_low, begin, narrow_block, 0)
        term = jnp.dot(basis_block, spectral_block, preferred_element_type=jnp.float32).astype(jnp.bfloat16)
        term = lax.optimization_barrier(term)
        return totals + term.astype(jnp.float32)
    update = lax.fori_loop(0, N_NARROW, basis_step, jnp.zeros((KL, KR), jnp.float32))
    return (moment_new, second_new, update.astype(jnp.bfloat16))
```

```python
import functools
import jax
import jax.numpy as jnp
from jax import lax
from jax.experimental import pallas as pl
from jax.experimental.pallas import tpu as pltpu
from jax.sharding import Mesh, PartitionSpec as P

STEP = 10

beta_first = 0.95
beta_second = 0.95
epsilon = 1e-08

AXES = ("x", "zl", "zh", "y", "core")
SIZES = (4, 8, 2, 4, 2)
BF16 = jnp.bfloat16
F32 = jnp.float32


def swap(value, axis, offset):
    size = dict(zip(AXES, SIZES))[axis]
    return lax.ppermute(value, axis, [(i, i ^ offset) for i in range(size)])


def pick_tiles(index, source, rows, cols, grid):
    down, across = grid

    def kernel(index_ref, source_ref, out_ref):
        for t in range(down * across):
            r, c = divmod(t, across)
            out_ref[r * rows : (r + 1) * rows, c * cols : (c + 1) * cols] = source_ref[index_ref[t]]

    return pl.pallas_call(
        kernel,
        out_shape=jax.ShapeDtypeStruct((down * rows, across * cols), source.dtype),
        in_specs=[
            pl.BlockSpec(memory_space=pltpu.SMEM),
            pl.BlockSpec(memory_space=pltpu.VMEM),
        ],
        out_specs=pl.BlockSpec(memory_space=pltpu.VMEM),
        compiler_params=pltpu.CompilerParams(vmem_limit_bytes=16 * 2**20),
        cost_estimate=pl.CostEstimate(
            flops=0, bytes_accessed=4 * down * rows * across * cols, transcendentals=0
        ),
    )(index, source)


def gather_line(value, axis):
    for offset in (4, 2, 1):
        value = jnp.concatenate([value, swap(value, "zl", offset)], axis=axis)
    return value


def shards(grad, moment, second, left_basis, right_basis):
    rows, cols = grad.shape
    x = lax.axis_index("x")
    zl = lax.axis_index("zl")
    zh = lax.axis_index("zh")
    y = lax.axis_index("y")
    core = lax.axis_index("core")
    y1, y0 = y // 2, y % 2
    x1, x0 = x // 2, x % 2

    moment_new = beta_first * moment + (1.0 - beta_first) * grad.astype(F32)
    both = jnp.concatenate([grad, moment_new.astype(BF16)], axis=0)

    tiles = jnp.stack([right_basis, swap(right_basis, "zh", 1)], axis=0)
    tiles = jnp.stack([tiles] + [swap(tiles, "y", k) for k in (1, 2, 3)], axis=0)
    tiles = tiles.reshape(2, 2, 2, rows, cols)
    parts = []
    for ox in range(4):
        want_zh = (x1 ^ (ox // 2)) ^ zh
        want_y1 = (x0 ^ (ox % 2)) ^ y1
        part = lax.dynamic_slice(
            tiles, (want_y1, 0, want_zh, 0, 0), (1, 2, 1, rows, cols)
        ).reshape(2, rows, cols)
        parts.append(part if ox == 0 else swap(part, "x", ox))
    parts = jnp.stack(parts, axis=0)
    parts = jnp.stack([parts, swap(parts, "core", 1)], axis=0)
    source = parts.reshape(32, rows // 2, cols)
    index = []
    for p in range(8):
        o = ((p & 1) << 2) | (p & 2) | (p >> 2)
        want = zl ^ o
        for ox in range(4):
            oc = ((want >> 1) & 1) ^ core
            oy0 = (want >> 2) ^ y0
            index.append(((oc * 4 + ox) * 2 + oy0) * 2 + (want & 1))
    right = pick_tiles(jnp.stack(index).astype(jnp.int32), source, rows // 2, cols, (8, 4))

    left = gather_line(left_basis, 0)
    left = jnp.concatenate([left] + [swap(left, "x", k) for k in (1, 2, 3)], axis=0)
    index = []
    for oc in range(2):
        for oy in range(4):
            for ozh in range(2):
                for half in range(2):
                    block = ((zh ^ ozh) * 8 + (y ^ oy) * 2 + (core ^ oc)) * 2 + half
                    o = (block % 8) ^ zl
                    p = ((o & 1) << 2) | (o & 2) | (o >> 2)
                    index.append(((block // 8) ^ x) * 8 + p)
    left_rows, left_width = left_basis.shape
    left = pick_tiles(
        jnp.stack(index).astype(jnp.int32),
        left.reshape(32, left_rows, left_width),
        left_rows,
        left_width,
        (32, 1),
    )

    both = gather_line(both, 1)
    partial = jnp.dot(both, right, preferred_element_type=F32)
    total = partial[:, :cols]
    for k in (1, 2, 3):
        piece = partial[:, k * cols : (k + 1) * cols].astype(BF16)
        total = total + swap(piece, "x", k).astype(F32)
    total = total.astype(BF16)
    rotated = jnp.concatenate([total[:rows], total[rows:]], axis=1)

    rotated = jnp.concatenate([rotated, swap(rotated, "zh", 1)], axis=0)
    rotated = jnp.concatenate([rotated] + [swap(rotated, "y", k) for k in (1, 2, 3)], axis=0)
    rotated = jnp.concatenate([rotated, swap(rotated, "core", 1)], axis=0)
    rot = lax.dot_general(
        left, rotated, (((0,), (0,)), ((), ())), preferred_element_type=F32
    )
    first, other = rot[:, :cols], rot[:, cols:]
    second_new = beta_second * second + (1.0 - beta_second) * first * first
    bias_first = 1.0 - beta_first**STEP
    bias_second = 1.0 - beta_second**STEP
    normed = (other / bias_first / (jnp.sqrt(second_new / bias_second) + epsilon)).astype(BF16)

    normed = jnp.concatenate([normed] + [swap(normed, "x", k) for k in (1, 2, 3)], axis=1)
    spectral = lax.dot_general(
        normed, right, (((1,), (1,)), ((), ())), preferred_element_type=F32
    )
    for offset in (1, 2, 4):
        half = spectral.shape[1] // 2
        sent = swap(spectral[:, half:].astype(BF16), "zl", offset)
        spectral = spectral[:, :half] + sent.astype(F32)
    spectral = spectral.astype(BF16)

    update = jnp.dot(left, spectral, preferred_element_type=F32)
    half = update.shape[0] // 2
    update = update[:half] + swap(update[half:].astype(BF16), "core", 1).astype(F32)
    quarter = half // 4
    total = update[:quarter]
    for k in (1, 2, 3):
        piece = update[k * quarter : (k + 1) * quarter].astype(BF16)
        total = total + swap(piece, "y", k).astype(F32)
    update = total[:rows] + swap(total[rows:].astype(BF16), "zh", 1).astype(F32)
    return (moment_new, second_new, update.astype(BF16))


def solution(mesh):
    fine = Mesh(mesh.devices.reshape(SIZES), AXES)
    spec = P(("zh", "y", "core"), ("x", "zl"))
    left_spec = P(("x", "zl"), ("zh", "y", "core"))
    return jax.shard_map(
        shards,
        mesh=fine,
        in_specs=(spec, spec, spec, left_spec, spec),
        out_specs=(spec, spec, spec),
        check_vma=False,
    )
```

```python
import jax
import jax.numpy as jnp
from jax import lax
from jax.experimental import pallas as pl
from jax.experimental.pallas import tpu as pltpu
from jax.sharding import Mesh, PartitionSpec as P

STEP = 10

beta_first = 0.95
beta_second = 0.95
epsilon = 1e-08

AXES = ("x", "zl", "zh", "y", "core")
SIZES = (4, 8, 2, 4, 2)
BF16 = jnp.bfloat16
F32 = jnp.float32


def swap(value, axis, offset):
    size = dict(zip(AXES, SIZES))[axis]
    return lax.ppermute(value, axis, [(i, i ^ offset) for i in range(size)])


def exchange(blocks, axis):
    return lax.all_to_all(blocks, axis, 0, 0, tiled=True)


def spread(value, axis):
    return exchange(jnp.broadcast_to(value[None], (4,) + value.shape), axis)


def place(index, sources, shape, size, moves, vmem):
    def kernel(index_ref, *refs):
        out_ref = refs[-1]
        for n, (source, lead, row, col, out_col) in enumerate(moves):
            tile = refs[source][lead + (pl.ds(row * size, size), pl.ds(col * size, size))]
            to = pl.multiple_of(index_ref[n] * size, size)
            out_ref[pl.ds(to, size), out_col * size : (out_col + 1) * size] = tile

    in_vmem = pl.BlockSpec(memory_space=pltpu.VMEM)
    nbytes = 4 * shape[0] * shape[1]
    return pl.pallas_call(
        kernel,
        out_shape=jax.ShapeDtypeStruct(shape, BF16),
        in_specs=[pl.BlockSpec(memory_space=pltpu.SMEM)] + [in_vmem] * len(sources),
        out_specs=in_vmem,
        compiler_params=pltpu.CompilerParams(vmem_limit_bytes=vmem),
        cost_estimate=pl.CostEstimate(flops=0, bytes_accessed=nbytes, transcendentals=0),
    )(index, *sources)


def reversed_bits(o):
    return ((o & 1) << 2) | (o & 2) | (o >> 2)


def shards(grad, moment, second, left_basis, right_basis):
    rows, cols = grad.shape
    x = lax.axis_index("x")
    zl = lax.axis_index("zl")
    zh = lax.axis_index("zh")
    y = lax.axis_index("y")
    core = lax.axis_index("core")
    barrier = lax.optimization_barrier

    moment_new = beta_first * moment + (1.0 - beta_first) * grad.astype(F32)
    line = jnp.concatenate(
        [grad, moment_new.astype(BF16), left_basis[:, :cols], left_basis[:, cols:]], axis=0
    )
    line, basis = barrier((line, right_basis))

    line = jnp.concatenate([line, swap(line, "zl", 4)], axis=1)
    basis = lax.all_gather(basis, "zh")
    line, basis = barrier((line, basis))

    line = jnp.concatenate([line, swap(line, "zl", 2)], axis=1)
    basis = spread(basis, "y")
    basis = basis.reshape(2, 2, 2, rows, cols).transpose(2, 0, 1, 3, 4)
    basis = basis.reshape(4, 2, rows, cols)
    line, basis = barrier((line, basis))

    line = jnp.concatenate([line, swap(line, "zl", 1)], axis=1)
    basis = exchange(basis, "x")
    basis = [basis, swap(basis, "core", 1)]
    index, moves = [], []
    for oc in range(2):
        for ox in range(4):
            for y0 in range(2):
                for half in range(2):
                    owner = y0 * 4 + (core ^ oc) * 2 + half
                    index.append(reversed_bits(owner ^ zl))
                    moves.append((oc, (ox, y0), half, 0, ox))
    right = place(
        jnp.stack(index).astype(jnp.int32), basis, (8 * cols, 4 * cols), cols, moves, 4 * 2**20
    )

    partial = jnp.dot(line[: 2 * rows], right, preferred_element_type=F32).astype(BF16)
    left, partial = barrier((line[2 * rows :], partial))
    partial = partial.reshape(2 * rows, 4, cols).transpose(1, 0, 2)
    total = jnp.sum(exchange(partial, "x").astype(F32), axis=0).astype(BF16)
    rotated = jnp.concatenate([total[:rows], total[rows:]], axis=1)

    left = [left] + [swap(left, "x", k) for k in (1, 3, 2)]
    rotated = jnp.concatenate([rotated, swap(rotated, "zh", 1)], axis=0)
    rotated, *left = barrier((rotated, *left))
    index, moves = [], []
    for number, ox in enumerate((0, 1, 3, 2)):
        for p in range(8):
            block = (x ^ ox) * 8 + (zl ^ reversed_bits(p))
            n = block // 2
            place_of = ((((n & 1) ^ core) * 4 + ((n >> 1) & 3)) * 2 + ((n >> 3) ^ zh)) * 2
            for half in range(2):
                index.append(place_of + (block & 1))
                moves.append((number, (), half, p, half))
    rotated = spread(rotated, "y").reshape(8 * rows, 2 * cols)
    left = place(
        jnp.stack(index).astype(jnp.int32), left, (32 * cols, 2 * cols), cols, moves, 8 * 2**20
    )
    other = swap(rotated, "core", 1)
    contract_rows = (((0,), (0,)), ((), ()))
    rot = lax.dot_general(
        left[: 8 * rows], rotated, contract_rows, preferred_element_type=F32
    ) + lax.dot_general(left[8 * rows :], other, contract_rows, preferred_element_type=F32)
    first, other = rot[:, :cols], rot[:, cols:]
    second_new = beta_second * second + (1.0 - beta_second) * first * first
    bias_first = 1.0 - beta_first**STEP
    bias_second = 1.0 - beta_second**STEP
    normed = (other / bias_first / (jnp.sqrt(second_new / bias_second) + epsilon)).astype(BF16)

    normed = spread(normed, "x").transpose(1, 0, 2).reshape(rows, 4 * cols)
    spectral = lax.dot_general(
        normed, right, (((1,), (1,)), ((), ())), preferred_element_type=F32
    )
    for offset in (1, 2, 4):
        half = spectral.shape[1] // 2
        sent = swap(spectral[:, half:].astype(BF16), "zl", offset)
        spectral = spectral[:, :half] + sent.astype(F32)
    spectral = spectral.astype(BF16)

    kept = barrier(jnp.dot(left[: 8 * rows], spectral, preferred_element_type=F32))
    sent = jnp.dot(left[8 * rows :], spectral, preferred_element_type=F32).astype(BF16)
    update = (kept + swap(sent, "core", 1).astype(F32)).astype(BF16)
    update = exchange(update.reshape(4, 2 * rows, cols), "y")
    update = jnp.sum(update.astype(F32), axis=0)
    update = update[:rows] + swap(update[rows:].astype(BF16), "zh", 1).astype(F32)
    return (moment_new, second_new, update.astype(BF16))


def solution(mesh):
    fine = Mesh(mesh.devices.reshape(SIZES), AXES)
    spec = P(("zh", "y", "core"), ("x", "zl"))
    left_spec = P(("x", "zl"), ("zh", "y", "core"))
    return jax.shard_map(
        shards,
        mesh=fine,
        in_specs=(spec, spec, spec, left_spec, spec),
        out_specs=(spec, spec, spec),
        check_vma=False,
    )
```

```python
import jax
import jax.numpy as jnp
from jax import lax
from jax.experimental import pallas as pl
from jax.experimental.pallas import tpu as pltpu
from jax.sharding import Mesh, PartitionSpec as P

STEP = 10

beta_first = 0.95
beta_second = 0.95
epsilon = 1e-08

AXES = ("x", "zl", "zh", "y", "core")
SIZES = (4, 8, 2, 4, 2)
BF16 = jnp.bfloat16
F32 = jnp.float32


def swap(value, axis, offset):
    size = dict(zip(AXES, SIZES))[axis]
    return lax.ppermute(value, axis, [(i, i ^ offset) for i in range(size)])


def exchange(blocks, axis):
    return lax.all_to_all(blocks, axis, 0, 0, tiled=True)


def spread(value, axis):
    return exchange(jnp.broadcast_to(value[None], (4,) + value.shape), axis)


def place(index, sources, shape, size, moves, vmem):
    def kernel(index_ref, *refs):
        out_ref = refs[-1]
        for n, (source, lead, row, col, out_col) in enumerate(moves):
            tile = refs[source][lead + (pl.ds(row * size, size), pl.ds(col * size, size))]
            to = pl.multiple_of(index_ref[n] * size, size)
            out_ref[pl.ds(to, size), out_col * size : (out_col + 1) * size] = tile

    in_vmem = pl.BlockSpec(memory_space=pltpu.VMEM)
    nbytes = 4 * shape[0] * shape[1]
    return pl.pallas_call(
        kernel,
        out_shape=jax.ShapeDtypeStruct(shape, BF16),
        in_specs=[pl.BlockSpec(memory_space=pltpu.SMEM)] + [in_vmem] * len(sources),
        out_specs=in_vmem,
        compiler_params=pltpu.CompilerParams(vmem_limit_bytes=vmem),
        cost_estimate=pl.CostEstimate(flops=0, bytes_accessed=nbytes, transcendentals=0),
    )(index, *sources)


def reversed_bits(o):
    return ((o & 1) << 2) | (o & 2) | (o >> 2)


def shards(grad, moment, second, left_basis, right_basis):
    rows, cols = grad.shape
    x = lax.axis_index("x")
    zl = lax.axis_index("zl")
    zh = lax.axis_index("zh")
    y = lax.axis_index("y")
    core = lax.axis_index("core")
    barrier = lax.optimization_barrier

    moment_new = beta_first * moment + (1.0 - beta_first) * grad.astype(F32)
    line = jnp.concatenate([grad, moment_new.astype(BF16)], axis=0)
    line, basis, left = barrier((line, right_basis, left_basis))

    line = jnp.concatenate([line, swap(line, "zl", 4)], axis=1)
    basis = lax.all_gather(lax.all_gather(basis, "zh"), "core", axis=1)
    line, basis, left = barrier((line, basis, left))

    line = jnp.concatenate([line, swap(line, "zl", 2)], axis=1)
    left = jnp.concatenate([left, swap(left, "zl", 4)], axis=0)
    basis = spread(basis, "y")
    basis = basis.reshape(2, 2, 2, 2, rows, cols).transpose(2, 0, 1, 3, 4, 5)
    basis = basis.reshape(4, 4, rows, cols)
    line, basis, left = barrier((line, basis, left))

    line = jnp.concatenate([line, swap(line, "zl", 1)], axis=1)
    left = jnp.concatenate([left, swap(left, "zl", 2)], axis=0)
    basis = exchange(basis, "x")
    index, other_index, moves = [], [], []
    for block in range(4):
        for half in range(2):
            owner = block * 2 + half
            for ox in range(4):
                index.append(reversed_bits(owner ^ zl))
                other_index.append((owner & 3) * 2 + ((owner ^ zl) >> 2))
                moves.append((0, (ox, block), half, 0, ox))
    shape = (8 * cols, 4 * cols)
    right = place(jnp.stack(index).astype(jnp.int32), [basis], shape, cols, moves, 4 * 2**20)
    right_back = place(
        jnp.stack(other_index).astype(jnp.int32), [basis], shape, cols, moves, 4 * 2**20
    )

    partial = jnp.dot(line, right, preferred_element_type=F32).astype(BF16)
    left, partial = barrier((left, partial))
    left = jnp.concatenate([left, swap(left, "zl", 1)], axis=0)
    partial = partial.reshape(2 * rows, 4, cols).transpose(1, 0, 2)
    total = jnp.sum(exchange(partial, "x").astype(F32), axis=0).astype(BF16)
    rotated = jnp.concatenate([total[:rows], total[rows:]], axis=1)
    left, rotated = barrier((left, rotated))

    left = [left] + [swap(left, "x", k) for k in (1, 3)]
    rotated = jnp.concatenate([rotated, swap(rotated, "zh", 1)], axis=0)
    rotated, *left = barrier((rotated, *left))
    left.append(swap(left[0], "x", 2))
    index, moves = [], []
    for number, ox in enumerate((0, 1, 3, 2)):
        for p in range(8):
            block = (x ^ ox) * 8 + (zl ^ reversed_bits(p))
            n = block // 2
            place_of = ((((n & 1) ^ core) * 4 + ((n >> 1) & 3)) * 2 + ((n >> 3) ^ zh)) * 2
            for half in range(2):
                index.append(place_of + (block & 1))
                moves.append((number, (), p, half, half))
    rotated = spread(rotated, "y").reshape(8 * rows, 2 * cols)
    rotated, *left = barrier((rotated, *left))
    left = place(
        jnp.stack(index).astype(jnp.int32), left, (32 * cols, 2 * cols), cols, moves, 8 * 2**20
    )
    other = swap(rotated, "core", 1)
    contract_rows = (((0,), (0,)), ((), ()))
    rot = lax.dot_general(
        left[: 8 * rows], rotated, contract_rows, preferred_element_type=F32
    ) + lax.dot_general(left[8 * rows :], other, contract_rows, preferred_element_type=F32)
    first, other = rot[:, :cols], rot[:, cols:]
    second_new = beta_second * second + (1.0 - beta_second) * first * first
    bias_first = 1.0 - beta_first**STEP
    bias_second = 1.0 - beta_second**STEP
    normed = (other / bias_first / (jnp.sqrt(second_new / bias_second) + epsilon)).astype(BF16)

    normed = spread(normed, "x").transpose(1, 0, 2).reshape(rows, 4 * cols)
    spectral = lax.dot_general(
        normed, right_back, (((1,), (1,)), ((), ())), preferred_element_type=F32
    )
    spectral = spectral.astype(BF16).reshape(rows, 4, 2 * cols).transpose(1, 0, 2)
    spectral = lax.all_to_all(
        spectral, "zl", 0, 0, tiled=True, axis_index_groups=[[0, 1, 2, 3], [4, 5, 6, 7]]
    )
    spectral = jnp.sum(spectral.astype(F32), axis=0)
    sent = swap(spectral[:, cols:].astype(BF16), "zl", 4)
    spectral = (spectral[:, :cols] + sent.astype(F32)).astype(BF16)

    kept = barrier(jnp.dot(left[: 8 * rows], spectral, preferred_element_type=F32))
    sent = jnp.dot(left[8 * rows :], spectral, preferred_element_type=F32).astype(BF16)
    update = (kept + swap(sent, "core", 1).astype(F32)).astype(BF16)
    update = exchange(update.reshape(4, 2 * rows, cols), "y")
    update = jnp.sum(update.astype(F32), axis=0)
    update = update[:rows] + swap(update[rows:].astype(BF16), "zh", 1).astype(F32)
    return (moment_new, second_new, update.astype(BF16))


def solution(mesh):
    fine = Mesh(mesh.devices.reshape(SIZES), AXES)
    spec = P(("zh", "y", "core"), ("x", "zl"))
    left_spec = P(("x", "zl"), ("zh", "y", "core"))
    return jax.shard_map(
        shards,
        mesh=fine,
        in_specs=(spec, spec, spec, left_spec, spec),
        out_specs=(spec, spec, spec),
        check_vma=False,
    )
```

```python
import jax
import jax.numpy as jnp
from jax import lax
from jax.experimental import pallas as pl
from jax.experimental.pallas import tpu as pltpu
from jax.experimental.layout import Layout, with_layout_constraint
from jax.sharding import Mesh, PartitionSpec as P

STEP = 10

beta_first = 0.95
beta_second = 0.95
epsilon = 1e-08

AXES = ("x", "z2", "z10", "zh", "y", "core")
SIZES = (4, 2, 4, 2, 4, 2)
BF16 = jnp.bfloat16
F32 = jnp.float32


def swap(value, axis, offset):
    size = dict(zip(AXES, SIZES))[axis]
    return lax.ppermute(value, axis, [(i, i ^ offset) for i in range(size)])


def exchange(blocks, axis):
    return lax.all_to_all(blocks, axis, 0, 0, tiled=True)


def spread(value, axis):
    return exchange(jnp.broadcast_to(value[None], (4,) + value.shape), axis)


def place(index, sources, shape, size, moves, vmem):
    def kernel(index_ref, *refs):
        out_ref = refs[-1]
        for n, (source, lead, row, col, out_col) in enumerate(moves):
            tile = refs[source][lead + (pl.ds(row * size, size), pl.ds(col * size, size))]
            to = pl.multiple_of(index_ref[n] * size, size)
            out_ref[pl.ds(to, size), out_col * size : (out_col + 1) * size] = tile

    in_vmem = pl.BlockSpec(memory_space=pltpu.VMEM)
    nbytes = 4 * shape[0] * shape[1]
    return pl.pallas_call(
        kernel,
        out_shape=jax.ShapeDtypeStruct(shape, BF16),
        in_specs=[pl.BlockSpec(memory_space=pltpu.SMEM)] + [in_vmem] * len(sources),
        out_specs=in_vmem,
        compiler_params=pltpu.CompilerParams(vmem_limit_bytes=vmem),
        cost_estimate=pl.CostEstimate(flops=0, bytes_accessed=nbytes, transcendentals=0),
    )(index, *sources)


OFFSETS = (0, 4, 2, 6, 1, 5, 3, 7)


def place_in_line(o):
    return ((o & 1) << 2) | (o & 2) | (o >> 2)


def shards(grad, moment, second, left_basis, right_basis):
    rows, cols = grad.shape
    x = lax.axis_index("x")
    z2 = lax.axis_index("z2")
    zl = z2 * 4 + lax.axis_index("z10")
    zh = lax.axis_index("zh")
    core = lax.axis_index("core")
    barrier = lax.optimization_barrier

    moment_new = beta_first * moment + (1.0 - beta_first) * grad.astype(F32)

    line = jnp.concatenate([grad, moment_new.astype(BF16), right_basis], axis=1)
    line = with_layout_constraint(line, Layout(major_to_minor=(0, 1)))
    line, left_basis = barrier((line, left_basis))
    left = jnp.concatenate([left_basis, swap(left_basis, "z2", 1)], axis=0)
    other = swap(line, "zh", 1)
    line = jnp.stack([jnp.where(zh == 0, line, other), jnp.where(zh == 0, other, line)])
    line, left = barrier((line, left))

    left = jnp.concatenate([left, swap(left, "z10", 2)], axis=0)
    left = jnp.concatenate([left, swap(left, "z10", 1)], axis=0)
    line = spread(line, "y")
    line, left = barrier((line, left))
    other = swap(line, "core", 1)

    basis = jnp.stack([line[..., 2 * cols :], other[..., 2 * cols :]])
    basis = basis.reshape(2, 2, 2, 2, rows, cols).transpose(3, 1, 0, 2, 4, 5)
    basis = basis.reshape(4, 4, rows, cols)
    basis = exchange(basis, "x")
    index, moves = [], []
    for block in range(4):
        for half in range(2):
            owner = (block % 2) * 4 + (core ^ (block // 2)) * 2 + half
            for ox in range(4):
                index.append(place_in_line(owner ^ zl))
                moves.append((0, (ox, block), half, 0, ox))
    index = jnp.stack(index).astype(jnp.int32)
    right = place(index, [basis], (8 * cols, 4 * cols), cols, moves, 4 * 2**20)

    lefts = [left] + [swap(left, "x", k) for k in (1, 3, 2)]
    index, moves = [], []
    for number, ox in enumerate((0, 1, 3, 2)):
        for p in range(8):
            block = (x ^ ox) * 8 + (zl ^ OFFSETS[p])
            n = block // 2
            to = ((((n & 1) ^ core) * 4 + ((n >> 1) & 3)) * 2 + (n >> 3)) * 2 + (block & 1)
            for half in range(2):
                index.append(to)
                moves.append((number, (), p, half, half))
    index = jnp.stack(index).astype(jnp.int32)
    left = place(index, lefts, (32 * cols, 2 * cols), cols, moves, 8 * 2**20)

    contract_rows = (((0,), (0,)), ((), ()))
    line = line[..., : 2 * cols].reshape(8 * rows, 2 * cols)
    other = other[..., : 2 * cols].reshape(8 * rows, 2 * cols)
    pair = lax.dot_general(
        left[: 8 * rows], line, contract_rows, preferred_element_type=F32
    ) + lax.dot_general(left[8 * rows :], other, contract_rows, preferred_element_type=F32)
    pair = pair.astype(BF16)
    pair = jnp.concatenate([pair[:, :cols], pair[:, cols:]], axis=0)

    pair = jnp.concatenate([pair, swap(pair, "z2", 1)], axis=1)
    pair = jnp.concatenate([pair, swap(pair, "z10", 2)], axis=1)
    pair = jnp.concatenate([pair, swap(pair, "z10", 1)], axis=1)
    pair = jnp.dot(pair, right, preferred_element_type=F32).astype(BF16)
    pair = pair.reshape(2 * rows, 4, cols).transpose(1, 0, 2)
    pair = jnp.sum(exchange(pair, "x").astype(F32), axis=0)
    first, other = pair[:rows], pair[rows:]
    second_new = beta_second * second + (1.0 - beta_second) * first * first
    bias_first = 1.0 - beta_first**STEP
    bias_second = 1.0 - beta_second**STEP
    normed = (other / bias_first / (jnp.sqrt(second_new / bias_second) + epsilon)).astype(BF16)

    normed = spread(normed, "x").transpose(1, 0, 2).reshape(rows, 4 * cols)
    spectral = lax.dot_general(
        normed, right, (((1,), (1,)), ((), ())), preferred_element_type=F32
    )
    for offset in (1, 2):
        half = spectral.shape[1] // 2
        sent = swap(spectral[:, half:].astype(BF16), "z10", offset)
        spectral = spectral[:, :half] + sent.astype(F32)
    spectral = spectral.astype(BF16)
    mine, others = spectral[:, :cols], spectral[:, cols:]
    spectral = jnp.concatenate(
        [jnp.where(z2 == 0, mine, others), jnp.where(z2 == 0, others, mine)], axis=1
    )

    kept = barrier(jnp.dot(left[: 8 * rows], spectral, preferred_element_type=F32))
    sent = jnp.dot(left[8 * rows :], spectral, preferred_element_type=F32).astype(BF16)
    update = (kept + swap(sent, "core", 1).astype(F32)).astype(BF16)
    update = exchange(update.reshape(4, 2 * rows, 2 * cols), "y")
    update = jnp.sum(update.astype(F32), axis=0).astype(BF16)
    update = update.reshape(2, rows, 2, cols).transpose(0, 2, 1, 3).reshape(4, rows, cols)
    update = jnp.sum(exchange(update, ("zh", "z2")).astype(F32), axis=0)
    return (moment_new, second_new, update.astype(BF16))


def solution(mesh):
    fine = Mesh(mesh.devices.reshape(SIZES), AXES)
    spec = P(("zh", "y", "core"), ("x", "z2", "z10"))
    left_spec = P(("x", "z2", "z10"), ("zh", "y", "core"))
    return jax.shard_map(
        shards,
        mesh=fine,
        in_specs=(spec, spec, spec, left_spec, spec),
        out_specs=(spec, spec, spec),
        check_vma=False,
    )
```

```python
import jax
import jax.numpy as jnp
from jax import lax
from jax.experimental import pallas as pl
from jax.experimental.pallas import tpu as pltpu
from jax.sharding import Mesh, PartitionSpec as P

STEP = 10

beta_first = 0.95
beta_second = 0.95
epsilon = 1e-08

AXES = ("x", "zl", "zh", "y", "core")
SIZES = (4, 8, 2, 4, 2)
BF16 = jnp.bfloat16
F32 = jnp.float32


def swap(value, axis, offset):
    size = dict(zip(AXES, SIZES))[axis]
    return lax.ppermute(value, axis, [(i, i ^ offset) for i in range(size)])


def exchange(blocks, axis):
    return lax.all_to_all(blocks, axis, 0, 0, tiled=True)


def spread(value, axis):
    return exchange(jnp.broadcast_to(value[None], (4,) + value.shape), axis)


def place(index, sources, shape, size, moves, vmem):
    def kernel(index_ref, *refs):
        out_ref = refs[-1]
        for n, (source, lead, row, col, out_col) in enumerate(moves):
            tile = refs[source][lead + (pl.ds(row * size, size), pl.ds(col * size, size))]
            to = pl.multiple_of(index_ref[n] * size, size)
            out_ref[pl.ds(to, size), out_col * size : (out_col + 1) * size] = tile

    in_vmem = pl.BlockSpec(memory_space=pltpu.VMEM)
    nbytes = 4 * shape[0] * shape[1]
    return pl.pallas_call(
        kernel,
        out_shape=jax.ShapeDtypeStruct(shape, BF16),
        in_specs=[pl.BlockSpec(memory_space=pltpu.SMEM)] + [in_vmem] * len(sources),
        out_specs=in_vmem,
        compiler_params=pltpu.CompilerParams(vmem_limit_bytes=vmem),
        cost_estimate=pl.CostEstimate(flops=0, bytes_accessed=nbytes, transcendentals=0),
    )(index, *sources)


def reversed_bits(o):
    return ((o & 1) << 2) | (o & 2) | (o >> 2)


def shards(grad, moment, second, left_basis, right_basis):
    rows, cols = grad.shape
    x = lax.axis_index("x")
    zl = lax.axis_index("zl")
    zh = lax.axis_index("zh")
    y = lax.axis_index("y")
    core = lax.axis_index("core")
    barrier = lax.optimization_barrier

    moment_new = beta_first * moment + (1.0 - beta_first) * grad.astype(F32)
    line = jnp.concatenate(
        [grad, moment_new.astype(BF16), left_basis[:, :cols], left_basis[:, cols:]], axis=0
    )
    line, basis = barrier((line, right_basis))

    line = jnp.concatenate([line, swap(line, "zl", 4)], axis=1)
    basis = lax.all_gather(basis, "zh")
    line, basis = barrier((line, basis))

    line = jnp.concatenate([line, swap(line, "zl", 2)], axis=1)
    basis = lax.all_gather(basis, "y")
    basis = basis.reshape(2, 2, 2, rows, cols).transpose(2, 0, 1, 3, 4)
    basis = basis.reshape(4, 2, rows, cols)
    line, basis = barrier((line, basis))

    line = jnp.concatenate([line, swap(line, "zl", 1)], axis=1)
    basis = exchange(basis, "x")
    basis = [basis, swap(basis, "core", 1)]
    index, moves = [], []
    for oc in range(2):
        for ox in range(4):
            for y0 in range(2):
                for half in range(2):
                    owner = y0 * 4 + (core ^ oc) * 2 + half
                    index.append(reversed_bits(owner ^ zl))
                    moves.append((oc, (ox, y0), half, 0, ox))
    right = place(
        jnp.stack(index).astype(jnp.int32), basis, (8 * cols, 4 * cols), cols, moves, 4 * 2**20
    )

    partial = jnp.dot(line[: 2 * rows], right, preferred_element_type=F32).astype(BF16)
    left, partial = barrier((line[2 * rows :], partial))
    partial = partial.reshape(2 * rows, 4, cols).transpose(1, 0, 2)
    total = jnp.sum(exchange(partial, "x").astype(F32), axis=0).astype(BF16)
    rotated = jnp.concatenate([total[:rows], total[rows:]], axis=1)

    left = [left] + [swap(left, "x", k) for k in (1, 3, 2)]
    rotated = jnp.concatenate([rotated, swap(rotated, "zh", 1)], axis=0)
    rotated, *left = barrier((rotated, *left))
    index, moves = [], []
    for number, ox in enumerate((0, 1, 3, 2)):
        for p in range(8):
            block = (x ^ ox) * 8 + (zl ^ reversed_bits(p))
            n = block // 2
            place_of = ((((n & 1) ^ core) * 4 + ((n >> 1) & 3)) * 2 + ((n >> 3) ^ zh)) * 2
            for half in range(2):
                index.append(place_of + (block & 1))
                moves.append((number, (), half, p, half))
    left = place(
        jnp.stack(index).astype(jnp.int32), left, (32 * cols, 2 * cols), cols, moves, 8 * 2**20
    )
    rotated = spread(rotated, "y").reshape(8 * rows, 2 * cols)
    rotated, left = barrier((rotated, left))
    other = swap(rotated, "core", 1)
    contract_rows = (((0,), (0,)), ((), ()))
    rot = lax.dot_general(
        left[: 8 * rows], rotated, contract_rows, preferred_element_type=F32
    ) + lax.dot_general(left[8 * rows :], other, contract_rows, preferred_element_type=F32)
    first, other = rot[:, :cols], rot[:, cols:]
    second_new = beta_second * second + (1.0 - beta_second) * first * first
    bias_first = 1.0 - beta_first**STEP
    bias_second = 1.0 - beta_second**STEP
    normed = (other / bias_first / (jnp.sqrt(second_new / bias_second) + epsilon)).astype(BF16)

    normed = spread(normed, "x").transpose(1, 0, 2).reshape(rows, 4 * cols)
    spectral = lax.dot_general(
        normed, right, (((1,), (1,)), ((), ())), preferred_element_type=F32
    )
    for offset in (1, 2, 4):
        half = spectral.shape[1] // 2
        sent = swap(spectral[:, half:].astype(BF16), "zl", offset)
        spectral = spectral[:, :half] + sent.astype(F32)
    spectral = spectral.astype(BF16)

    kept = barrier(jnp.dot(left[: 8 * rows], spectral, preferred_element_type=F32))
    sent = jnp.dot(left[8 * rows :], spectral, preferred_element_type=F32).astype(BF16)
    update = (kept + swap(sent, "core", 1).astype(F32)).astype(BF16)
    update = exchange(update.reshape(4, 2 * rows, cols), "y")
    update = jnp.sum(update.astype(F32), axis=0)
    update = update[:rows] + swap(update[rows:].astype(BF16), "zh", 1).astype(F32)
    return (moment_new, second_new, update.astype(BF16))


def solution(mesh):
    fine = Mesh(mesh.devices.reshape(SIZES), AXES)
    spec = P(("zh", "y", "core"), ("x", "zl"))
    left_spec = P(("x", "zl"), ("zh", "y", "core"))
    return jax.shard_map(
        shards,
        mesh=fine,
        in_specs=(spec, spec, spec, left_spec, spec),
        out_specs=(spec, spec, spec),
        check_vma=False,
    )
```

```python
import jax
import jax.numpy as jnp
from jax import lax
from jax.experimental import pallas as pl
from jax.experimental.pallas import tpu as pltpu
from jax.sharding import Mesh, PartitionSpec as P

STEP = 10

beta_first = 0.95
beta_second = 0.95
epsilon = 1e-08

AXES = ("x", "zl", "zh", "y", "core")
SIZES = (4, 8, 2, 4, 2)
BF16 = jnp.bfloat16
F32 = jnp.float32


def swap(value, axis, offset):
    size = dict(zip(AXES, SIZES))[axis]
    return lax.ppermute(value, axis, [(i, i ^ offset) for i in range(size)])


def exchange(blocks, axis):
    return lax.all_to_all(blocks, axis, 0, 0, tiled=True)


def spread(value, axis):
    return exchange(jnp.broadcast_to(value[None], (4,) + value.shape), axis)


def place(index, sources, shape, size, moves, vmem):
    def kernel(index_ref, *refs):
        out_ref = refs[-1]
        for n, (source, lead, row, col, out_col) in enumerate(moves):
            tile = refs[source][lead + (pl.ds(row * size, size), pl.ds(col * size, size))]
            to = pl.multiple_of(index_ref[n] * size, size)
            out_ref[pl.ds(to, size), out_col * size : (out_col + 1) * size] = tile

    in_vmem = pl.BlockSpec(memory_space=pltpu.VMEM)
    nbytes = 4 * shape[0] * shape[1]
    return pl.pallas_call(
        kernel,
        out_shape=jax.ShapeDtypeStruct(shape, BF16),
        in_specs=[pl.BlockSpec(memory_space=pltpu.SMEM)] + [in_vmem] * len(sources),
        out_specs=in_vmem,
        compiler_params=pltpu.CompilerParams(vmem_limit_bytes=vmem),
        cost_estimate=pl.CostEstimate(flops=0, bytes_accessed=nbytes, transcendentals=0),
    )(index, *sources)


def reversed_bits(o):
    return ((o & 1) << 2) | (o & 2) | (o >> 2)


def shards(grad, moment, second, left_basis, right_basis):
    rows, cols = grad.shape
    x = lax.axis_index("x")
    zl = lax.axis_index("zl")
    zh = lax.axis_index("zh")
    y = lax.axis_index("y")
    core = lax.axis_index("core")
    barrier = lax.optimization_barrier

    moment_new = beta_first * moment + (1.0 - beta_first) * grad.astype(F32)
    line = jnp.concatenate(
        [grad, moment_new.astype(BF16), left_basis[:, :cols], left_basis[:, cols:]], axis=0
    )
    line, basis = barrier((line, right_basis))

    line = jnp.concatenate([line, swap(line, "zl", 4)], axis=1)
    basis = lax.all_gather(basis, "zh")
    line, basis = barrier((line, basis))

    line = jnp.concatenate([line, swap(line, "zl", 2)], axis=1)
    basis = lax.all_gather(basis, "y")
    basis = basis.reshape(2, 2, 2, rows, cols).transpose(2, 0, 1, 3, 4)
    basis = basis.reshape(4, 2, rows, cols)
    line, basis = barrier((line, basis))

    line = jnp.concatenate([line, swap(line, "zl", 1)], axis=1)
    basis = exchange(basis, "x")
    basis = [basis, swap(basis, "core", 1)]
    index, moves = [], []
    for oc in range(2):
        for ox in range(4):
            for y0 in range(2):
                for half in range(2):
                    owner = y0 * 4 + (core ^ oc) * 2 + half
                    index.append(reversed_bits(owner ^ zl))
                    moves.append((oc, (ox, y0), half, 0, ox))
    right = place(
        jnp.stack(index).astype(jnp.int32), basis, (8 * cols, 4 * cols), cols, moves, 4 * 2**20
    )

    partial = jnp.dot(line[: 2 * rows], right, preferred_element_type=F32).astype(BF16)
    left, partial = barrier((line[2 * rows :], partial))
    partial = partial.reshape(2 * rows, 4, cols).transpose(1, 0, 2)
    total = jnp.sum(exchange(partial, "x").astype(F32), axis=0).astype(BF16)
    rotated = jnp.concatenate([total[:rows], total[rows:]], axis=1)

    left = [left] + [swap(left, "x", k) for k in (1, 3, 2)]
    other = swap(rotated, "zh", 1)
    rotated = jnp.concatenate(
        [jnp.where(zh == 0, rotated, other), jnp.where(zh == 0, other, rotated)], axis=0
    )
    rotated, *left = barrier((rotated, *left))
    index, moves = [], []
    for number, ox in enumerate((0, 1, 3, 2)):
        for p in range(8):
            block = (x ^ ox) * 8 + (zl ^ reversed_bits(p))
            n = block // 2
            place_of = ((((n & 1) ^ core) * 4 + ((n >> 1) & 3)) * 2 + (n >> 3)) * 2
            for half in range(2):
                index.append(place_of + (block & 1))
                moves.append((number, (), half, p, half))
    left = place(
        jnp.stack(index).astype(jnp.int32), left, (32 * cols, 2 * cols), cols, moves, 8 * 2**20
    )
    rotated = spread(rotated, "y").reshape(8 * rows, 2 * cols)
    rotated, left = barrier((rotated, left))
    other = swap(rotated, "core", 1)
    contract_rows = (((0,), (0,)), ((), ()))
    rot = lax.dot_general(
        left[: 8 * rows], rotated, contract_rows, preferred_element_type=F32
    ) + lax.dot_general(left[8 * rows :], other, contract_rows, preferred_element_type=F32)
    first, other = rot[:, :cols], rot[:, cols:]
    second_new = beta_second * second + (1.0 - beta_second) * first * first
    bias_first = 1.0 - beta_first**STEP
    bias_second = 1.0 - beta_second**STEP
    normed = (other / bias_first / (jnp.sqrt(second_new / bias_second) + epsilon)).astype(BF16)

    normed = spread(normed, "x").transpose(1, 0, 2).reshape(rows, 4 * cols)
    spectral = lax.dot_general(
        normed, right, (((1,), (1,)), ((), ())), preferred_element_type=F32
    )
    for offset in (1, 2, 4):
        half = spectral.shape[1] // 2
        sent = swap(spectral[:, half:].astype(BF16), "zl", offset)
        spectral = spectral[:, :half] + sent.astype(F32)
    spectral = spectral.astype(BF16)

    kept = barrier(jnp.dot(left[: 8 * rows], spectral, preferred_element_type=F32))
    sent = jnp.dot(left[8 * rows :], spectral, preferred_element_type=F32).astype(BF16)
    update = (kept + swap(sent, "core", 1).astype(F32)).astype(BF16)
    update = exchange(update.reshape(8, rows, cols), ("y", "zh"))
    update = jnp.sum(update.astype(F32), axis=0)
    return (moment_new, second_new, update.astype(BF16))


def solution(mesh):
    fine = Mesh(mesh.devices.reshape(SIZES), AXES)
    spec = P(("zh", "y", "core"), ("x", "zl"))
    left_spec = P(("x", "zl"), ("zh", "y", "core"))
    return jax.shard_map(
        shards,
        mesh=fine,
        in_specs=(spec, spec, spec, left_spec, spec),
        out_specs=(spec, spec, spec),
        check_vma=False,
    )
```

```python
import jax
import jax.numpy as jnp
from jax import lax
from jax.experimental import pallas as pl
from jax.experimental.pallas import tpu as pltpu
from jax.sharding import Mesh, PartitionSpec as P

STEP = 10

beta_first = 0.95
beta_second = 0.95
epsilon = 1e-08

AXES = ("x", "zl", "zh", "y", "core")
SIZES = (4, 8, 2, 4, 2)
BF16 = jnp.bfloat16
F32 = jnp.float32


def swap(value, axis, offset):
    size = dict(zip(AXES, SIZES))[axis]
    return lax.ppermute(value, axis, [(i, i ^ offset) for i in range(size)])


def exchange(blocks, axis):
    return lax.all_to_all(blocks, axis, 0, 0, tiled=True)


def spread(value, axis):
    return exchange(jnp.broadcast_to(value[None], (4,) + value.shape), axis)


def place(index, sources, shape, size, moves, vmem):
    def kernel(index_ref, *refs):
        out_ref = refs[-1]
        for n, (source, lead, row, col, out_col) in enumerate(moves):
            tile = refs[source][lead + (pl.ds(row * size, size), pl.ds(col * size, size))]
            to = pl.multiple_of(index_ref[n] * size, size)
            out_ref[pl.ds(to, size), out_col * size : (out_col + 1) * size] = tile

    in_vmem = pl.BlockSpec(memory_space=pltpu.VMEM)
    nbytes = 4 * shape[0] * shape[1]
    return pl.pallas_call(
        kernel,
        out_shape=jax.ShapeDtypeStruct(shape, BF16),
        in_specs=[pl.BlockSpec(memory_space=pltpu.SMEM)] + [in_vmem] * len(sources),
        out_specs=in_vmem,
        compiler_params=pltpu.CompilerParams(vmem_limit_bytes=vmem),
        cost_estimate=pl.CostEstimate(flops=0, bytes_accessed=nbytes, transcendentals=0),
    )(index, *sources)


def begin(grad, moment, left_basis):
    rows, cols = grad.shape
    half = rows // 2

    def kernel(grad_ref, moment_ref, left_ref, moment_new_ref, line_ref, old_ref, sems):
        moves = [
            (grad_ref, line_ref.at[pl.ds(0, rows)]),
            (moment_ref, old_ref),
            (left_ref.at[:, pl.ds(0, cols)], line_ref.at[pl.ds(2 * rows, half)]),
            (left_ref.at[:, pl.ds(cols, cols)], line_ref.at[pl.ds(2 * rows + half, half)]),
        ]
        copies = [
            pltpu.make_async_copy(source, target, sems.at[n])
            for n, (source, target) in enumerate(moves)
        ]
        for copy in copies:
            copy.start()
        copies[0].wait()
        copies[1].wait()
        new = beta_first * old_ref[...] + (1.0 - beta_first) * line_ref[:rows].astype(F32)
        moment_new_ref[...] = new
        line_ref[rows : 2 * rows] = new.astype(BF16)
        copies[2].wait()
        copies[3].wait()

    in_hbm = pl.BlockSpec(memory_space=pltpu.HBM)
    in_vmem = pl.BlockSpec(memory_space=pltpu.VMEM)
    return pl.pallas_call(
        kernel,
        out_shape=(
            jax.ShapeDtypeStruct(moment.shape, F32),
            jax.ShapeDtypeStruct((3 * rows, cols), BF16),
        ),
        in_specs=[in_hbm] * 3,
        out_specs=(in_vmem, in_vmem),
        scratch_shapes=[pltpu.VMEM(moment.shape, F32), pltpu.SemaphoreType.DMA((4,))],
        cost_estimate=pl.CostEstimate(
            flops=3 * rows * cols, bytes_accessed=18 * rows * cols, transcendentals=0
        ),
    )(grad, moment, left_basis)


def reversed_bits(o):
    return ((o & 1) << 2) | (o & 2) | (o >> 2)


def shards(grad, moment, second, left_basis, right_basis):
    rows, cols = grad.shape
    x = lax.axis_index("x")
    zl = lax.axis_index("zl")
    zh = lax.axis_index("zh")
    y = lax.axis_index("y")
    core = lax.axis_index("core")
    barrier = lax.optimization_barrier

    moment_new, line = begin(grad, moment, left_basis)
    line, basis = barrier((line, right_basis))

    line = jnp.concatenate([line, swap(line, "zl", 4)], axis=1)
    basis = lax.all_gather(basis, "zh")
    line, basis = barrier((line, basis))

    line = jnp.concatenate([line, swap(line, "zl", 2)], axis=1)
    basis = lax.all_gather(basis, "y")
    basis = basis.reshape(2, 2, 2, rows, cols).transpose(2, 0, 1, 3, 4)
    basis = basis.reshape(4, 2, rows, cols)
    line, basis = barrier((line, basis))

    line = jnp.concatenate([line, swap(line, "zl", 1)], axis=1)
    basis = exchange(basis, "x")
    basis = [basis, swap(basis, "core", 1)]
    index, moves = [], []
    for oc in range(2):
        for ox in range(4):
            for y0 in range(2):
                for half in range(2):
                    owner = y0 * 4 + (core ^ oc) * 2 + half
                    index.append(reversed_bits(owner ^ zl))
                    moves.append((oc, (ox, y0), half, 0, ox))
    right = place(
        jnp.stack(index).astype(jnp.int32), basis, (8 * cols, 4 * cols), cols, moves, 4 * 2**20
    )

    partial = jnp.dot(line[: 2 * rows], right, preferred_element_type=F32).astype(BF16)
    left, partial = barrier((line[2 * rows :], partial))
    partial = partial.reshape(2 * rows, 4, cols).transpose(1, 0, 2)
    total = jnp.sum(exchange(partial, "x").astype(F32), axis=0).astype(BF16)
    rotated = jnp.concatenate([total[:rows], total[rows:]], axis=1)

    left = [left] + [swap(left, "x", k) for k in (1, 3, 2)]
    rotated = jnp.concatenate([rotated, swap(rotated, "zh", 1)], axis=0)
    rotated, *left = barrier((rotated, *left))
    index, moves = [], []
    for number, ox in enumerate((0, 1, 3, 2)):
        for p in range(8):
            block = (x ^ ox) * 8 + (zl ^ reversed_bits(p))
            n = block // 2
            place_of = ((((n & 1) ^ core) * 4 + ((n >> 1) & 3)) * 2 + ((n >> 3) ^ zh)) * 2
            for half in range(2):
                index.append(place_of + (block & 1))
                moves.append((number, (), half, p, half))
    left = place(
        jnp.stack(index).astype(jnp.int32), left, (32 * cols, 2 * cols), cols, moves, 8 * 2**20
    )
    rotated = spread(rotated, "y").reshape(8 * rows, 2 * cols)
    rotated, left = barrier((rotated, left))
    other = swap(rotated, "core", 1)
    contract_rows = (((0,), (0,)), ((), ()))
    rot = lax.dot_general(
        left[: 8 * rows], rotated, contract_rows, preferred_element_type=F32
    ) + lax.dot_general(left[8 * rows :], other, contract_rows, preferred_element_type=F32)
    first, other = rot[:, :cols], rot[:, cols:]
    second_new = beta_second * second + (1.0 - beta_second) * first * first
    bias_first = 1.0 - beta_first**STEP
    bias_second = 1.0 - beta_second**STEP
    normed = (other / bias_first / (jnp.sqrt(second_new / bias_second) + epsilon)).astype(BF16)

    normed = spread(normed, "x").transpose(1, 0, 2).reshape(rows, 4 * cols)
    spectral = lax.dot_general(
        normed, right, (((1,), (1,)), ((), ())), preferred_element_type=F32
    )
    for offset in (1, 2, 4):
        half = spectral.shape[1] // 2
        sent = swap(spectral[:, half:].astype(BF16), "zl", offset)
        spectral = spectral[:, :half] + sent.astype(F32)
    spectral = spectral.astype(BF16)

    kept = barrier(jnp.dot(left[: 8 * rows], spectral, preferred_element_type=F32))
    sent = jnp.dot(left[8 * rows :], spectral, preferred_element_type=F32).astype(BF16)
    update = (kept + swap(sent, "core", 1).astype(F32)).astype(BF16)
    update = exchange(update.reshape(4, 2 * rows, cols), "y")
    update = jnp.sum(update.astype(F32), axis=0)
    update = update[:rows] + swap(update[rows:].astype(BF16), "zh", 1).astype(F32)
    return (moment_new, second_new, update.astype(BF16))


def solution(mesh):
    fine = Mesh(mesh.devices.reshape(SIZES), AXES)
    spec = P(("zh", "y", "core"), ("x", "zl"))
    left_spec = P(("x", "zl"), ("zh", "y", "core"))
    return jax.shard_map(
        shards,
        mesh=fine,
        in_specs=(spec, spec, spec, left_spec, spec),
        out_specs=(spec, spec, spec),
        check_vma=False,
    )
```

```python
import jax
import jax.numpy as jnp
from jax import lax
from jax.experimental import pallas as pl
from jax.experimental.pallas import tpu as pltpu
from jax.sharding import Mesh, PartitionSpec as P

STEP = 10

beta_first = 0.95
beta_second = 0.95
epsilon = 1e-08

AXES = ("x", "zl", "zh", "y", "core")
SIZES = (4, 8, 2, 4, 2)
BF16 = jnp.bfloat16
F32 = jnp.float32


def swap(value, axis, offset):
    size = dict(zip(AXES, SIZES))[axis]
    return lax.ppermute(value, axis, [(i, i ^ offset) for i in range(size)])


def exchange(blocks, axis):
    return lax.all_to_all(blocks, axis, 0, 0, tiled=True)


def spread(value, axis):
    return exchange(jnp.broadcast_to(value[None], (4,) + value.shape), axis)


def place(index, sources, shape, size, moves, vmem):
    def kernel(index_ref, *refs):
        out_ref = refs[-1]
        for n, (source, lead, row, col, out_col) in enumerate(moves):
            tile = refs[source][lead + (pl.ds(row * size, size), pl.ds(col * size, size))]
            to = pl.multiple_of(index_ref[n] * size, size)
            out_ref[pl.ds(to, size), out_col * size : (out_col + 1) * size] = tile

    in_vmem = pl.BlockSpec(memory_space=pltpu.VMEM)
    nbytes = 4 * shape[0] * shape[1]
    return pl.pallas_call(
        kernel,
        out_shape=jax.ShapeDtypeStruct(shape, BF16),
        in_specs=[pl.BlockSpec(memory_space=pltpu.SMEM)] + [in_vmem] * len(sources),
        out_specs=in_vmem,
        compiler_params=pltpu.CompilerParams(vmem_limit_bytes=vmem),
        cost_estimate=pl.CostEstimate(flops=0, bytes_accessed=nbytes, transcendentals=0),
    )(index, *sources)


def reversed_bits(o):
    return ((o & 1) << 2) | (o & 2) | (o >> 2)


def shards(grad, moment, second, left_basis, right_basis):
    rows, cols = grad.shape
    x = lax.axis_index("x")
    zl = lax.axis_index("zl")
    zh = lax.axis_index("zh")
    y = lax.axis_index("y")
    core = lax.axis_index("core")
    barrier = lax.optimization_barrier

    moment_new = beta_first * moment + (1.0 - beta_first) * grad.astype(F32)
    line = jnp.concatenate(
        [grad, moment_new.astype(BF16), left_basis[:, :cols], left_basis[:, cols:]], axis=0
    )
    line, basis = barrier((line, right_basis))

    line = jnp.concatenate([line, swap(line, "zl", 4)], axis=1)
    other = swap(basis, "zh", 1)
    basis = jnp.stack([jnp.where(zh == 0, basis, other), jnp.where(zh == 0, other, basis)])

    line = jnp.concatenate([line, swap(line, "zl", 2)], axis=1)
    basis = lax.all_gather(basis, "y")
    basis = basis.reshape(2, 2, 2, rows, cols).transpose(2, 0, 1, 3, 4)
    basis = basis.reshape(4, 2, rows, cols)
    line, basis = barrier((line, basis))

    line = jnp.concatenate([line, swap(line, "zl", 1)], axis=1)
    basis = exchange(basis, "x")
    basis = [basis, swap(basis, "core", 1)]
    index, moves = [], []
    for oc in range(2):
        for ox in range(4):
            for y0 in range(2):
                for half in range(2):
                    owner = y0 * 4 + (core ^ oc) * 2 + half
                    index.append(reversed_bits(owner ^ zl))
                    moves.append((oc, (ox, y0), half, 0, ox))
    right = place(
        jnp.stack(index).astype(jnp.int32), basis, (8 * cols, 4 * cols), cols, moves, 4 * 2**20
    )

    partial = jnp.dot(line[: 2 * rows], right, preferred_element_type=F32).astype(BF16)
    left, partial = barrier((line[2 * rows :], partial))
    partial = partial.reshape(2 * rows, 4, cols).transpose(1, 0, 2)
    total = jnp.sum(exchange(partial, "x").astype(F32), axis=0).astype(BF16)
    rotated = jnp.concatenate([total[:rows], total[rows:]], axis=1)

    left = [left] + [swap(left, "x", k) for k in (1, 3, 2)]
    rotated = jnp.concatenate([rotated, swap(rotated, "zh", 1)], axis=0)
    rotated, *left = barrier((rotated, *left))
    index, moves = [], []
    for number, ox in enumerate((0, 1, 3, 2)):
        for p in range(8):
            block = (x ^ ox) * 8 + (zl ^ reversed_bits(p))
            n = block // 2
            place_of = ((((n & 1) ^ core) * 4 + ((n >> 1) & 3)) * 2 + ((n >> 3) ^ zh)) * 2
            for half in range(2):
                index.append(place_of + (block & 1))
                moves.append((number, (), half, p, half))
    left = place(
        jnp.stack(index).astype(jnp.int32), left, (32 * cols, 2 * cols), cols, moves, 8 * 2**20
    )
    rotated = spread(rotated, "y").reshape(8 * rows, 2 * cols)
    rotated, left = barrier((rotated, left))
    other = swap(rotated, "core", 1)
    contract_rows = (((0,), (0,)), ((), ()))
    rot = lax.dot_general(
        left[: 8 * rows], rotated, contract_rows, preferred_element_type=F32
    ) + lax.dot_general(left[8 * rows :], other, contract_rows, preferred_element_type=F32)
    first, other = rot[:, :cols], rot[:, cols:]
    second_new = beta_second * second + (1.0 - beta_second) * first * first
    bias_first = 1.0 - beta_first**STEP
    bias_second = 1.0 - beta_second**STEP
    normed = (other / bias_first / (jnp.sqrt(second_new / bias_second) + epsilon)).astype(BF16)

    normed = spread(normed, "x").transpose(1, 0, 2).reshape(rows, 4 * cols)
    spectral = lax.dot_general(
        normed, right, (((1,), (1,)), ((), ())), preferred_element_type=F32
    )
    for offset in (1, 2, 4):
        half = spectral.shape[1] // 2
        sent = swap(spectral[:, half:].astype(BF16), "zl", offset)
        spectral = spectral[:, :half] + sent.astype(F32)
    spectral = spectral.astype(BF16)

    kept = barrier(jnp.dot(left[: 8 * rows], spectral, preferred_element_type=F32))
    sent = jnp.dot(left[8 * rows :], spectral, preferred_element_type=F32).astype(BF16)
    update = (kept + swap(sent, "core", 1).astype(F32)).astype(BF16)
    update = exchange(update.reshape(4, 2 * rows, cols), "y")
    update = jnp.sum(update.astype(F32), axis=0)
    update = update[:rows] + swap(update[rows:].astype(BF16), "zh", 1).astype(F32)
    return (moment_new, second_new, update.astype(BF16))


def solution(mesh):
    fine = Mesh(mesh.devices.reshape(SIZES), AXES)
    spec = P(("zh", "y", "core"), ("x", "zl"))
    left_spec = P(("x", "zl"), ("zh", "y", "core"))
    return jax.shard_map(
        shards,
        mesh=fine,
        in_specs=(spec, spec, spec, left_spec, spec),
        out_specs=(spec, spec, spec),
        check_vma=False,
    )
```

```python
import jax
import jax.numpy as jnp
from jax import lax
from jax.experimental import pallas as pl
from jax.experimental.pallas import tpu as pltpu
from jax.sharding import Mesh, PartitionSpec as P

STEP = 10

beta_first = 0.95
beta_second = 0.95
epsilon = 1e-08

AXES = ("x", "zl", "zh", "y", "core")
SIZES = (4, 8, 2, 4, 2)
BF16 = jnp.bfloat16
F32 = jnp.float32


def swap(value, axis, offset):
    size = dict(zip(AXES, SIZES))[axis]
    return lax.ppermute(value, axis, [(i, i ^ offset) for i in range(size)])


def exchange(blocks, axis):
    return lax.all_to_all(blocks, axis, 0, 0, tiled=True)


def spread(value, axis):
    return exchange(jnp.broadcast_to(value[None], (4,) + value.shape), axis)


def place(index, sources, shape, size, moves, vmem):
    def kernel(index_ref, *refs):
        out_ref = refs[-1]
        for n, (source, lead, row, col, out_col) in enumerate(moves):
            tile = refs[source][lead + (pl.ds(row * size, size), pl.ds(col * size, size))]
            to = pl.multiple_of(index_ref[n] * size, size)
            out_ref[pl.ds(to, size), out_col * size : (out_col + 1) * size] = tile

    in_vmem = pl.BlockSpec(memory_space=pltpu.VMEM)
    nbytes = 4 * shape[0] * shape[1]
    return pl.pallas_call(
        kernel,
        out_shape=jax.ShapeDtypeStruct(shape, BF16),
        in_specs=[pl.BlockSpec(memory_space=pltpu.SMEM)] + [in_vmem] * len(sources),
        out_specs=in_vmem,
        compiler_params=pltpu.CompilerParams(vmem_limit_bytes=vmem),
        cost_estimate=pl.CostEstimate(flops=0, bytes_accessed=nbytes, transcendentals=0),
    )(index, *sources)


def begin(grad, moment, left_basis):
    rows, cols = grad.shape
    half = rows // 2

    def kernel(grad_ref, moment_ref, left_ref, moment_new_ref, line_ref, old_ref, sems):
        moves = [
            (grad_ref, line_ref.at[pl.ds(0, rows)]),
            (moment_ref, old_ref),
            (left_ref.at[:, pl.ds(0, cols)], line_ref.at[pl.ds(2 * rows, half)]),
            (left_ref.at[:, pl.ds(cols, cols)], line_ref.at[pl.ds(2 * rows + half, half)]),
        ]
        copies = [
            pltpu.make_async_copy(source, target, sems.at[n])
            for n, (source, target) in enumerate(moves)
        ]
        for copy in copies:
            copy.start()
        copies[0].wait()
        copies[1].wait()
        new = beta_first * old_ref[...] + (1.0 - beta_first) * line_ref[:rows].astype(F32)
        moment_new_ref[...] = new
        line_ref[rows : 2 * rows] = new.astype(BF16)
        copies[2].wait()
        copies[3].wait()

    in_hbm = pl.BlockSpec(memory_space=pltpu.HBM)
    in_vmem = pl.BlockSpec(memory_space=pltpu.VMEM)
    return pl.pallas_call(
        kernel,
        out_shape=(
            jax.ShapeDtypeStruct(moment.shape, F32),
            jax.ShapeDtypeStruct((3 * rows, cols), BF16),
        ),
        in_specs=[in_hbm] * 3,
        out_specs=(in_vmem, in_vmem),
        scratch_shapes=[pltpu.VMEM(moment.shape, F32), pltpu.SemaphoreType.DMA((4,))],
        cost_estimate=pl.CostEstimate(
            flops=3 * rows * cols, bytes_accessed=18 * rows * cols, transcendentals=0
        ),
    )(grad, moment, left_basis)


def reversed_bits(o):
    return ((o & 1) << 2) | (o & 2) | (o >> 2)


def shards(grad, moment, second, left_basis, right_basis):
    rows, cols = grad.shape
    x = lax.axis_index("x")
    zl = lax.axis_index("zl")
    zh = lax.axis_index("zh")
    y = lax.axis_index("y")
    core = lax.axis_index("core")
    barrier = lax.optimization_barrier

    moment_new, line = begin(grad, moment, left_basis)
    line, basis = barrier((line, right_basis))

    line = jnp.concatenate([line, swap(line, "zl", 4)], axis=1)
    other = swap(basis, "zh", 1)
    basis = jnp.stack([jnp.where(zh == 0, basis, other), jnp.where(zh == 0, other, basis)])

    line = jnp.concatenate([line, swap(line, "zl", 2)], axis=1)
    basis = lax.all_gather(basis, "y")
    basis = basis.reshape(2, 2, 2, rows, cols).transpose(2, 0, 1, 3, 4)
    basis = basis.reshape(4, 2, rows, cols)
    line, basis = barrier((line, basis))

    line = jnp.concatenate([line, swap(line, "zl", 1)], axis=1)
    basis = exchange(basis, "x")
    basis = [basis, swap(basis, "core", 1)]
    index, moves = [], []
    for oc in range(2):
        for ox in range(4):
            for y0 in range(2):
                for half in range(2):
                    owner = y0 * 4 + (core ^ oc) * 2 + half
                    index.append(reversed_bits(owner ^ zl))
                    moves.append((oc, (ox, y0), half, 0, ox))
    right = place(
        jnp.stack(index).astype(jnp.int32), basis, (8 * cols, 4 * cols), cols, moves, 4 * 2**20
    )

    partial = jnp.dot(line[: 2 * rows], right, preferred_element_type=F32).astype(BF16)
    left, partial = barrier((line[2 * rows :], partial))
    partial = partial.reshape(2 * rows, 4, cols).transpose(1, 0, 2)
    total = jnp.sum(exchange(partial, "x").astype(F32), axis=0).astype(BF16)
    rotated = jnp.concatenate([total[:rows], total[rows:]], axis=1)

    left = [left] + [swap(left, "x", k) for k in (1, 3, 2)]
    rotated = jnp.concatenate([rotated, swap(rotated, "zh", 1)], axis=0)
    rotated, *left = barrier((rotated, *left))
    index, moves = [], []
    for number, ox in enumerate((0, 1, 3, 2)):
        for p in range(8):
            block = (x ^ ox) * 8 + (zl ^ reversed_bits(p))
            n = block // 2
            place_of = ((((n & 1) ^ core) * 4 + ((n >> 1) & 3)) * 2 + ((n >> 3) ^ zh)) * 2
            for half in range(2):
                index.append(place_of + (block & 1))
                moves.append((number, (), half, p, half))
    left = place(
        jnp.stack(index).astype(jnp.int32), left, (32 * cols, 2 * cols), cols, moves, 8 * 2**20
    )
    rotated = spread(rotated, "y").reshape(8 * rows, 2 * cols)
    rotated, left = barrier((rotated, left))
    other = swap(rotated, "core", 1)
    contract_rows = (((0,), (0,)), ((), ()))
    rot = lax.dot_general(
        left[: 8 * rows], rotated, contract_rows, preferred_element_type=F32
    ) + lax.dot_general(left[8 * rows :], other, contract_rows, preferred_element_type=F32)
    first, other = rot[:, :cols], rot[:, cols:]
    second_new = beta_second * second + (1.0 - beta_second) * first * first
    bias_first = 1.0 - beta_first**STEP
    bias_second = 1.0 - beta_second**STEP
    normed = (other / bias_first / (jnp.sqrt(second_new / bias_second) + epsilon)).astype(BF16)

    normed = spread(normed, "x").transpose(1, 0, 2).reshape(rows, 4 * cols)
    spectral = lax.dot_general(
        normed, right, (((1,), (1,)), ((), ())), preferred_element_type=F32
    )
    for offset in (1, 2, 4):
        half = spectral.shape[1] // 2
        sent = swap(spectral[:, half:].astype(BF16), "zl", offset)
        spectral = spectral[:, :half] + sent.astype(F32)
    spectral = spectral.astype(BF16)

    kept = barrier(jnp.dot(left[: 8 * rows], spectral, preferred_element_type=F32))
    sent = jnp.dot(left[8 * rows :], spectral, preferred_element_type=F32).astype(BF16)
    update = (kept + swap(sent, "core", 1).astype(F32)).astype(BF16)
    update = exchange(update.reshape(4, 2 * rows, cols), "y")
    update = jnp.sum(update.astype(F32), axis=0)
    update = update[:rows] + swap(update[rows:].astype(BF16), "zh", 1).astype(F32)
    return (moment_new, second_new, update.astype(BF16))


def solution(mesh):
    fine = Mesh(mesh.devices.reshape(SIZES), AXES)
    spec = P(("zh", "y", "core"), ("x", "zl"))
    left_spec = P(("x", "zl"), ("zh", "y", "core"))
    return jax.shard_map(
        shards,
        mesh=fine,
        in_specs=(spec, spec, spec, left_spec, spec),
        out_specs=(spec, spec, spec),
        check_vma=False,
    )
```

```python
import jax
import jax.numpy as jnp
from jax import lax
from jax.experimental import pallas as pl
from jax.experimental.pallas import tpu as pltpu
from jax.sharding import Mesh, PartitionSpec as P

STEP = 10

beta_first = 0.95
beta_second = 0.95
epsilon = 1e-08

AXES = ("x", "zl", "zh", "y", "core")
SIZES = (4, 8, 2, 4, 2)
BF16 = jnp.bfloat16
F32 = jnp.float32


def swap(value, axis, offset):
    size = dict(zip(AXES, SIZES))[axis]
    return lax.ppermute(value, axis, [(i, i ^ offset) for i in range(size)])


def exchange(blocks, axis):
    return lax.all_to_all(blocks, axis, 0, 0, tiled=True)


def spread(value, axis):
    return exchange(jnp.broadcast_to(value[None], (4,) + value.shape), axis)


def place(index, sources, shape, size, moves, vmem):
    def kernel(index_ref, *refs):
        out_ref = refs[-1]
        for n, (source, lead, row, col, out_col) in enumerate(moves):
            tile = refs[source][lead + (pl.ds(row * size, size), pl.ds(col * size, size))]
            to = pl.multiple_of(index_ref[n] * size, size)
            out_ref[pl.ds(to, size), out_col * size : (out_col + 1) * size] = tile

    in_vmem = pl.BlockSpec(memory_space=pltpu.VMEM)
    nbytes = 4 * shape[0] * shape[1]
    return pl.pallas_call(
        kernel,
        out_shape=jax.ShapeDtypeStruct(shape, BF16),
        in_specs=[pl.BlockSpec(memory_space=pltpu.SMEM)] + [in_vmem] * len(sources),
        out_specs=in_vmem,
        compiler_params=pltpu.CompilerParams(vmem_limit_bytes=vmem),
        cost_estimate=pl.CostEstimate(flops=0, bytes_accessed=nbytes, transcendentals=0),
    )(index, *sources)


def reversed_bits(o):
    return ((o & 1) << 2) | (o & 2) | (o >> 2)


def shards(grad, moment, second, left_basis, right_basis):
    rows, cols = grad.shape
    x = lax.axis_index("x")
    zl = lax.axis_index("zl")
    zh = lax.axis_index("zh")
    y = lax.axis_index("y")
    core = lax.axis_index("core")
    barrier = lax.optimization_barrier

    moment_new = beta_first * moment + (1.0 - beta_first) * grad.astype(F32)
    line = jnp.concatenate(
        [grad, moment_new.astype(BF16), left_basis[:, :cols], left_basis[:, cols:]], axis=0
    )
    line, basis = barrier((line, right_basis))

    line = jnp.concatenate([line, swap(line, "zl", 4)], axis=1)
    other = swap(basis, "zh", 1)
    basis = jnp.stack([jnp.where(zh == 0, basis, other), jnp.where(zh == 0, other, basis)])

    line = jnp.concatenate([line, swap(line, "zl", 2)], axis=1)
    basis = lax.all_gather(basis, "y")
    basis = basis.reshape(2, 2, 2, rows, cols).transpose(2, 0, 1, 3, 4)
    basis = basis.reshape(4, 2, rows, cols)
    line, basis = barrier((line, basis))

    line = jnp.concatenate([line, swap(line, "zl", 1)], axis=1)
    basis = exchange(basis, "x")
    basis = [basis, swap(basis, "core", 1)]
    index, moves = [], []
    for oc in range(2):
        for ox in range(4):
            for y0 in range(2):
                for half in range(2):
                    owner = y0 * 4 + (core ^ oc) * 2 + half
                    index.append(reversed_bits(owner ^ zl))
                    moves.append((oc, (ox, y0), half, 0, ox))
    right = place(
        jnp.stack(index).astype(jnp.int32), basis, (8 * cols, 4 * cols), cols, moves, 4 * 2**20
    )

    partial = jnp.dot(line[: 2 * rows], right, preferred_element_type=F32).astype(BF16)
    left, partial = barrier((line[2 * rows :], partial))
    partial = partial.reshape(2 * rows, 4, cols).transpose(1, 0, 2)
    total = jnp.sum(exchange(partial, "x").astype(F32), axis=0).astype(BF16)
    rotated = jnp.concatenate([total[:rows], total[rows:]], axis=1)

    left = [left] + [swap(left, "x", k) for k in (1, 3, 2)]
    rotated = jnp.concatenate([rotated, swap(rotated, "zh", 1)], axis=0)
    rotated, left[1], left[3] = barrier((rotated, left[1], left[3]))
    index, moves = [], []
    for number, ox in enumerate((0, 1, 3, 2)):
        for p in range(8):
            block = (x ^ ox) * 8 + (zl ^ reversed_bits(p))
            n = block // 2
            place_of = ((((n & 1) ^ core) * 4 + ((n >> 1) & 3)) * 2 + ((n >> 3) ^ zh)) * 2
            for half in range(2):
                index.append(place_of + (block & 1))
                moves.append((number, (), half, p, half))
    left = place(
        jnp.stack(index).astype(jnp.int32), left, (32 * cols, 2 * cols), cols, moves, 8 * 2**20
    )
    rotated = spread(rotated, "y").reshape(8 * rows, 2 * cols)
    rotated, left = barrier((rotated, left))
    other = swap(rotated, "core", 1)
    contract_rows = (((0,), (0,)), ((), ()))
    rot = lax.dot_general(
        left[: 8 * rows], rotated, contract_rows, preferred_element_type=F32
    ) + lax.dot_general(left[8 * rows :], other, contract_rows, preferred_element_type=F32)
    first, other = rot[:, :cols], rot[:, cols:]
    second_new = beta_second * second + (1.0 - beta_second) * first * first
    bias_first = 1.0 - beta_first**STEP
    bias_second = 1.0 - beta_second**STEP
    normed = (other / bias_first / (jnp.sqrt(second_new / bias_second) + epsilon)).astype(BF16)

    normed = spread(normed, "x").transpose(1, 0, 2).reshape(rows, 4 * cols)
    spectral = lax.dot_general(
        normed, right, (((1,), (1,)), ((), ())), preferred_element_type=F32
    )
    for offset in (1, 2, 4):
        half = spectral.shape[1] // 2
        sent = swap(spectral[:, half:].astype(BF16), "zl", offset)
        spectral = spectral[:, :half] + sent.astype(F32)
    spectral = spectral.astype(BF16)

    kept = barrier(jnp.dot(left[: 8 * rows], spectral, preferred_element_type=F32))
    sent = jnp.dot(left[8 * rows :], spectral, preferred_element_type=F32).astype(BF16)
    update = (kept + swap(sent, "core", 1).astype(F32)).astype(BF16)
    update = exchange(update.reshape(4, 2 * rows, cols), "y")
    update = jnp.sum(update.astype(F32), axis=0)
    update = update[:rows] + swap(update[rows:].astype(BF16), "zh", 1).astype(F32)
    return (moment_new, second_new, update.astype(BF16))


def solution(mesh):
    fine = Mesh(mesh.devices.reshape(SIZES), AXES)
    spec = P(("zh", "y", "core"), ("x", "zl"))
    left_spec = P(("x", "zl"), ("zh", "y", "core"))
    return jax.shard_map(
        shards,
        mesh=fine,
        in_specs=(spec, spec, spec, left_spec, spec),
        out_specs=(spec, spec, spec),
        check_vma=False,
    )
```
